32 devices in a mesh: room: 2 (over y), gx: 16 (over z, x, core).
Axes of the slice: x: 2, y: 2, z: 4, core: 2. Of those that a mesh axis runs over, the one named last changes fastest.
Arguments:
- pressure: float32 [256, 256, 256], P(('room', 'gx')), parts along dimension 0, may hold values from -6 to 6
- previous: float32 [256, 256, 256], P(('room', 'gx')), parts along dimension 0, may hold values from -6 to 6
- materials: int32 [256, 256, 256], P(('room', 'gx')), parts along dimension 0, may hold values from 0 to 15
- admittance: float32 [32], P('room'), parts along dimension 0, may hold values from 0.05 to 1
- absorption: float32 [32], P('room'), parts along dimension 0, may hold values from 0.01 to 0.3
- source_cell: int32 [2], P('room'), parts along dimension 0, may hold values from 0 to 8388607
- signal: float32 [8], P('room'), parts along dimension 0, may hold values from -6 to 6
- receivers: int32 [128], P('room'), parts along dimension 0, may hold values from 0 to 8388607, as said below
Outputs:
- pressure_out: float32 [256, 256, 256], P(('room', 'gx')), parts along dimension 0
- previous_out: float32 [256, 256, 256], P(('room', 'gx')), parts along dimension 0
- readings: float32 [8, 64], P('room'), parts along dimension 0
The draws below stay inside these ranges and needn't reach their ends.
There are 2 independent parts, one for each index of `room`. The reference program is written for one: setup_inputs(seed, part) draws one part's arguments, and reference() takes and returns one part's arrays. A program takes and returns all parts, laid end to end along the dimension named above; each array names one. Nothing has to cross between parts.
Inputs may be any that keep to these rules, and one draw needn't show every extreme that they name: `receivers`: receiver r lies on a layer of the first dimension from (r mod (16)) * 8 to that plus 8 - 1.
All inputs are finite; a program needn't handle non-finite values.
Results may differ from the reference program's by a relative error of at most 0.00002.
Values sent between devices are 32-bit elements; how exact they have to be, the bound alone decides.
A program may use at most 64 MiB of HBM per device.

```python
import math
import jax
import jax.numpy as jnp

CX = 8
NY = 256
NZ = 256
STEPS = 4
MATS = 16
NX = 128
RECV = 64


def draw_receivers(key, part):
    key = jax.random.fold_in(key, 7)
    key_slab, key_row, key_col = jax.random.split(key, 3)
    ordinal = jnp.arange(RECV, dtype=jnp.int32)
    layer = ordinal % (NX // CX) * CX + jax.random.randint(key_slab, (RECV,), 0, CX, dtype=jnp.int32)
    row_y = jax.random.randint(key_row, (RECV,), 0, NY, dtype=jnp.int32)
    col_z = jax.random.randint(key_col, (RECV,), 0, NZ, dtype=jnp.int32)
    return ((layer * NY + row_y) * NZ + col_z).astype(jnp.int32)


def with_ends(drawn, key, low, largest):
    dims = drawn.shape
    index_at = [jax.random.randint(jax.random.fold_in(key, axis), (), 0, dims[axis]) for axis in range(len(dims))]
    drawn = drawn.at[tuple(index_at)].set(low)
    longest = dims.index(max(dims))
    index_at[longest] = (index_at[longest] + 1) % dims[longest]
    return drawn.at[tuple(index_at)].set(largest)


def block_levels(stream_key, extent, cuts, least, largest):
    factor_of = 1.0
    for dim, parts in cuts:
        heights = jax.random.uniform(jax.random.fold_in(jax.random.fold_in(stream_key, 6), dim), (parts,), jnp.float32, least / len(cuts), largest / len(cuts))
        factor_of = factor_of * jnp.repeat(jnp.exp(heights), extent[dim] // parts).reshape((-1,) + (1,) * (len(extent) - 1 - dim))
    return factor_of


def gaussian(rng, shape, deviation, most, cuts=(), kind=jnp.bfloat16):
    array = deviation * jax.random.normal(rng, shape, jnp.float32)
    if cuts:
        array = array * block_levels(rng, shape, cuts, -0.22, 0.18)
    return jnp.clip(array, -most, most).astype(kind)


def setup_inputs(seed: int = 0, part: int = 0) -> dict:
    streams_of = jax.random.split(jax.random.key(seed), 9)
    part_keys = jax.random.split(jax.random.fold_in(streams_of[8], part), 9)
    return {
        "pressure": gaussian(part_keys[0], (NX, NY, NZ), 1.0, 6.0, ((0, 16),), jnp.float32),
        "previous": gaussian(part_keys[1], (NX, NY, NZ), 1.0, 6.0, ((0, 16),), jnp.float32),
        "materials": with_ends(jax.random.randint(part_keys[2], (NX, NY, NZ), 0, MATS), jax.random.fold_in(part_keys[2], 1), 0, MATS - 1).astype(jnp.int32),
        "admittance": jnp.clip(jax.random.uniform(part_keys[3], (MATS,), jnp.float32, 0.05, 1.0), 0.05, 1.0),
        "absorption": jnp.clip(jnp.exp(jax.random.uniform(part_keys[4], (MATS,), jnp.float32, math.log(0.01), math.log(0.3))), 0.01, 0.3),
        "source_cell": jax.random.randint(part_keys[5], (1,), 0, NX * NY * NZ).astype(jnp.int32),
        "signal": gaussian(part_keys[6], (STEPS,), 1.0, 6.0, (), jnp.float32),
        "receivers": draw_receivers(jax.random.fold_in(jax.random.fold_in(streams_of[8], part), 71), part),
    }


courant = 0.5773502691896258
courant_sq = 1.0 / 3.0


def outside_count(start_x, slab_width, grid_x, size_y, size_z):
    coord_x = start_x + jnp.arange(slab_width)
    coord_y = jnp.arange(size_y)
    coord_z = jnp.arange(size_z)
    edge_x = ((coord_x == 0) | (coord_x == grid_x - 1)).astype(jnp.float32)
    edge_y = ((coord_y == 0) | (coord_y == size_y - 1)).astype(jnp.float32)
    edge_z = ((coord_z == 0) | (coord_z == size_z - 1)).astype(jnp.float32)
    return edge_x[:, None, None] + edge_y[None, :, None] + edge_z[None, None, :]


def neighbours(field):
    padded = jnp.pad(field, 1)
    summed = padded[2:, 1:-1, 1:-1] + padded[:-2, 1:-1, 1:-1]
    summed = summed + padded[1:-1, 2:, 1:-1] + padded[1:-1, :-2, 1:-1]
    summed = summed + padded[1:-1, 1:-1, 2:] + padded[1:-1, 1:-1, :-2]
    return summed


def reference(pressure, previous, materials, admittance, absorption, source_cell, signal, receivers):
    outside = outside_count(0, NX, NX, NY, NZ)
    loss_cell = 0.5 * courant * outside * admittance[materials] + absorption[materials]
    inside = 6.0 - outside
    source_flat = source_cell[0]
    source_x = source_flat // (NY * NZ)
    source_y = (source_flat // NZ) % NY
    source_z = source_flat % NZ
    samples = []
    for moment in range(STEPS):
        summed = neighbours(pressure)
        following = ((2.0 - courant_sq * inside) * pressure + courant_sq * summed - (1.0 - loss_cell) * previous) / (1.0 + loss_cell)
        following = following.at[source_x, source_y, source_z].add(signal[moment])
        samples.append(following.reshape(-1)[receivers])
        previous, pressure = pressure, following
    return pressure, previous, jnp.stack(samples)
```

```python
import functools

import jax
import jax.numpy as jnp
from jax import lax
from jax.experimental import pallas as pl
from jax.experimental.pallas import tpu as pltpu
from jax.sharding import PartitionSpec as P

courant = 0.5773502691896258
courant_sq = 1.0 / 3.0

STRIPS = 4


def kernel(
    groups,
    steps,
    adm_ref,
    abs_ref,
    source_ref,
    signal_ref,
    recv_ref,
    pressure_ref,
    previous_ref,
    materials_ref,
    field,
    readings_ref,
    mats,
    coef,
    halo,
    mine,
    gathered,
    load_sem,
    first_send,
    send_sem,
    halo_sem,
    gather_send,
    gather_recv,
):
    layers, size_y, size_z = pressure_ref.shape
    rows = size_y // STRIPS
    receivers = recv_ref.shape[0]
    classes = adm_ref.shape[0]
    me = lax.axis_index("gx")
    start_x = me * layers
    has_left = me > 0
    has_right = me < groups - 1

    loads = [
        pltpu.make_async_copy(materials_ref, mats, load_sem.at[0]),
        pltpu.make_async_copy(pressure_ref, field.at[0], load_sem.at[1]),
        pltpu.make_async_copy(previous_ref, field.at[1], load_sem.at[2]),
    ]
    for load in loads:
        load.start()

    barrier = pltpu.get_barrier_semaphore()

    def greet(hop, carry):
        pl.semaphore_signal(barrier, inc=1, device_id={"gx": lax.rem(me + hop, groups)}, device_id_type=pl.DeviceIdType.MESH)
        return carry

    lax.fori_loop(1, groups, greet, 0)
    pl.semaphore_wait(barrier, groups - 1)

    def first_copy(side, strip):
        layer = layers - 1 if side == 0 else 0
        return pltpu.make_async_remote_copy(
            src_ref=pressure_ref.at[layer, pl.ds(strip * rows, rows), :],
            dst_ref=halo.at[0, side, strip],
            send_sem=first_send.at[side, strip],
            recv_sem=halo_sem.at[0, side, strip],
            device_id={"gx": me + 1 if side == 0 else me - 1},
            device_id_type=pl.DeviceIdType.MESH,
        )

    def step_copy(step, side, strip):
        layer = layers - 1 if side == 0 else 0
        return pltpu.make_async_remote_copy(
            src_ref=field.at[lax.rem(step + 1, 2), layer, pl.ds(pl.multiple_of(strip * rows, rows), rows), :],
            dst_ref=halo.at[step + 1, side, strip],
            send_sem=send_sem.at[step, side, strip],
            recv_sem=halo_sem.at[step + 1, side, strip],
            device_id={"gx": me + 1 if side == 0 else me - 1},
            device_id_type=pl.DeviceIdType.MESH,
        )

    for strip in range(STRIPS):
        pl.when(has_right)(lambda: first_copy(0, strip).start())
        pl.when(has_left)(lambda: first_copy(1, strip).start())

    lane = lax.broadcasted_iota(jnp.int32, (8, 128), 1)
    outside_lane = lane // classes
    class_lane = lane - outside_lane * classes
    adm_lane = jnp.zeros((8, 128), jnp.float32)
    abs_lane = jnp.zeros((8, 128), jnp.float32)
    for m in range(classes):
        adm_lane = jnp.where(class_lane == m, adm_ref[m], adm_lane)
        abs_lane = jnp.where(class_lane == m, abs_ref[m], abs_lane)
    table = courant_sq / (1.0 + (0.5 * courant * outside_lane.astype(jnp.float32) * adm_lane + abs_lane))

    loads[0].wait()
    block = 64
    table_block = jnp.broadcast_to(table[0:1], (block, 128))

    def fill(i, carry):
        layer = i // (size_y // block)
        row0 = pl.multiple_of(lax.rem(i, size_y // block) * block, block)
        at_x = start_x + layer
        edge_x = jnp.where((at_x == 0) | (at_x == groups * layers - 1), classes, 0)
        row = row0 + lax.broadcasted_iota(jnp.int32, (block, 128), 0)
        edge_xy = edge_x + jnp.where((row == 0) | (row == size_y - 1), classes, 0)
        for part in range(size_z // 128):
            cols = pl.ds(part * 128, 128)
            index = mats[layer, pl.ds(row0, block), cols] + edge_xy
            col = part * 128 + lax.broadcasted_iota(jnp.int32, (block, 128), 1)
            index = index + jnp.where((col == 0) | (col == size_z - 1), classes, 0)
            coef[layer, pl.ds(row0, block), cols] = jnp.take_along_axis(table_block, index, axis=1, mode="promise_in_bounds")
        return carry

    lax.fori_loop(0, layers * (size_y // block), fill, 0)
    loads[1].wait()
    loads[2].wait()

    source = source_ref[0]
    source_x = source // (size_y * size_z) - start_x
    source_y = (source // size_z) % size_y
    source_z = source % size_z

    row_id = lax.broadcasted_iota(jnp.int32, (rows, size_z), 0)
    col_id = lax.broadcasted_iota(jnp.int32, (rows, size_z), 1)
    mine[...] = jnp.zeros(mine.shape, jnp.float32)
    wide = mine.shape[1]
    mine_row = lax.broadcasted_iota(jnp.int32, mine.shape, 0)
    mine_col = lax.broadcasted_iota(jnp.int32, mine.shape, 1)
    lane_row = lax.broadcasted_iota(jnp.int32, (1, size_z), 1)

    def one_layer(step, now, then, strip, layer, low, high):
        row0 = pl.multiple_of(strip * rows, rows)
        here = pl.ds(row0, rows)
        c = field[now, layer, here, :]
        above = field[now, layer, pl.ds(jnp.maximum(row0 - 1, 0), 1), :]
        below = field[now, layer, pl.ds(jnp.minimum(row0 + rows, size_y - 1), 1), :]
        total = low + high
        total = total + jnp.where(row_id == 0, above, pltpu.roll(c, 1, 0))
        total = total + jnp.where(row_id == rows - 1, below, pltpu.roll(c, rows - 1, 0))
        total = total + jnp.where(col_id == 0, c, pltpu.roll(c, 1, 1))
        total = total + jnp.where(col_id == size_z - 1, c, pltpu.roll(c, size_z - 1, 1))
        old = field[then, layer, here, :]
        following = old + coef[layer, here, :] * (total - 6.0 * old)
        push = jnp.where(source_x == layer, signal_ref[step], 0.0)
        push = jnp.where(lane_row == source_z, push, 0.0)
        following = following + jnp.where(row_id == source_y - row0, push, 0.0)
        field[then, layer, here, :] = following

    def strip_body(step, strip):
        now = lax.rem(step, 2)
        then = 1 - now
        here = pl.ds(pl.multiple_of(strip * rows, rows), rows)

        @pl.when(has_left)
        def _():
            pltpu.make_async_copy(halo.at[step, 0, strip], halo.at[step, 0, strip], halo_sem.at[step, 0, strip]).wait()

        @pl.when(has_right)
        def _():
            pltpu.make_async_copy(halo.at[step, 1, strip], halo.at[step, 1, strip], halo_sem.at[step, 1, strip]).wait()

        pl.when((step >= 2) & has_right)(lambda: step_copy(step - 2, 0, strip).wait_send())
        pl.when((step >= 2) & has_left)(lambda: step_copy(step - 2, 1, strip).wait_send())

        first = field[now, 0, here, :]
        last = field[now, layers - 1, here, :]
        low = jnp.where(has_left, halo[step, 0, strip], first)
        high = jnp.where(has_right, halo[step, 1, strip], last)
        one_layer(step, now, then, strip, 0, low, field[now, 1, here, :])
        one_layer(step, now, then, strip, layers - 1, field[now, layers - 2, here, :], high)

        pl.when((step < steps - 1) & has_right)(lambda: step_copy(step, 0, strip).start())
        pl.when((step < steps - 1) & has_left)(lambda: step_copy(step, 1, strip).start())

        for layer in range(1, layers - 1):
            one_layer(step, now, then, strip, layer, field[now, layer - 1, here, :], field[now, layer + 1, here, :])

    def step_body(step, carry):
        def inner(strip, c):
            strip_body(step, strip)
            return c

        lax.fori_loop(0, STRIPS, inner, 0)
        then = lax.rem(step + 1, 2)
        total = mine[...]
        for k in range(receivers // groups):
            slot = k * groups + me
            cell = recv_ref[slot]
            at_x = jnp.clip(cell // (size_y * size_z) - start_x, 0, layers - 1)
            at_y = (cell // size_z) % size_y
            at_z = cell % size_z
            line = field[then, at_x, pl.ds(at_y, 1), :]
            value = jnp.sum(jnp.where(lane_row == at_z, line, 0.0), axis=1, keepdims=True)
            total = total + jnp.where((mine_row == step) & (mine_col == slot), value, 0.0)
        mine[...] = total
        return carry

    lax.fori_loop(0, steps, step_body, 0)

    def gather_copy(hop):
        peer = lax.rem(me + hop, groups)
        return pltpu.make_async_remote_copy(
            src_ref=mine,
            dst_ref=gathered.at[hop],
            send_sem=gather_send.at[hop],
            recv_sem=gather_recv.at[hop],
            device_id={"gx": peer},
            device_id_type=pl.DeviceIdType.MESH,
        )

    def gather_start(hop, carry):
        gather_copy(hop).start()
        return carry

    lax.fori_loop(1, groups, gather_start, 0)

    for strip in range(STRIPS):
        pl.when(has_right)(lambda: first_copy(0, strip).wait_send())
        pl.when(has_left)(lambda: first_copy(1, strip).wait_send())
        pl.when(has_right)(lambda: step_copy(steps - 2, 0, strip).wait_send())
        pl.when(has_left)(lambda: step_copy(steps - 2, 1, strip).wait_send())

    def gather_add(hop, total):
        gather_copy(hop).wait()
        return total + gathered[hop]

    total = lax.fori_loop(1, groups, gather_add, mine[...])
    readings_ref[...] = total[0:steps, 0:receivers]


def local(pressure, previous, materials, admittance, absorption, source_cell, signal, receivers):
    layers, size_y, size_z = pressure.shape
    groups = lax.axis_size("gx")
    steps = signal.shape[0]
    wide = -(-receivers.shape[0] // 128) * 128
    rows = size_y // STRIPS
    smem = pl.BlockSpec(memory_space=pltpu.SMEM)
    vmem = pl.BlockSpec(memory_space=pltpu.VMEM)
    hbm = pl.BlockSpec(memory_space=pl.ANY)
    field, readings = pl.pallas_call(
        functools.partial(kernel, groups, steps),
        out_shape=(
            jax.ShapeDtypeStruct((2, layers, size_y, size_z), jnp.float32),
            jax.ShapeDtypeStruct((steps, receivers.shape[0]), jnp.float32),
        ),
        in_specs=[smem] * 5 + [hbm] * 3,
        out_specs=(vmem, vmem),
        scratch_shapes=[
            pltpu.VMEM((layers, size_y, size_z), jnp.int32),
            pltpu.VMEM((layers, size_y, size_z), jnp.float32),
            pltpu.VMEM((steps, 2, STRIPS, rows, size_z), jnp.float32),
            pltpu.VMEM((8, wide), jnp.float32),
            pltpu.VMEM((groups, 8, wide), jnp.float32),
            pltpu.SemaphoreType.DMA((3,)),
            pltpu.SemaphoreType.DMA((2, STRIPS)),
            pltpu.SemaphoreType.DMA((steps, 2, STRIPS)),
            pltpu.SemaphoreType.DMA((steps, 2, STRIPS)),
            pltpu.SemaphoreType.DMA((groups,)),
            pltpu.SemaphoreType.DMA((groups,)),
        ],
        compiler_params=pltpu.CompilerParams(
            collective_id=0, has_side_effects=True, vmem_limit_bytes=48 * 1024 * 1024
        ),
        name="steps",
    )(admittance, absorption, source_cell, signal, receivers, pressure, previous, materials)
    return field[steps % 2], field[(steps + 1) % 2], readings


def solution(mesh):
    slab = P(("room", "gx"), None, None)
    return jax.shard_map(
        local,
        mesh=mesh,
        in_specs=(slab, slab, slab, P("room"), P("room"), P("room"), P("room"), P("room")),
        out_specs=(slab, slab, P("room", None)),
        check_vma=False,
    )
```

```python
import functools

import jax
import jax.numpy as jnp
from jax import lax
from jax.experimental import pallas as pl
from jax.experimental.pallas import tpu as pltpu
from jax.sharding import PartitionSpec as P

courant = 0.5773502691896258
courant_sq = 1.0 / 3.0

STRIPS = 4
AHEAD = 2


def kernel(
    groups,
    steps,
    adm_hbm,
    abs_hbm,
    source_hbm,
    signal_hbm,
    recv_hbm,
    pressure_ref,
    previous_ref,
    materials_ref,
    field,
    readings_ref,
    adm_ref,
    abs_ref,
    source_ref,
    signal_ref,
    recv_ref,
    small_sem,
    mats,
    coef,
    halo,
    mine,
    gathered,
    load_sem,
    send_sem,
    halo_sem,
    gather_send,
    gather_recv,
):
    layers, size_y, size_z = pressure_ref.shape
    rows = size_y // STRIPS
    receivers = recv_ref.shape[0]
    classes = adm_ref.shape[0]
    me = lax.axis_index("gx")
    start_x = me * layers
    has_left = me > 0
    has_right = me < groups - 1

    def load(which, strip):
        source, target = ((pressure_ref, field.at[0]), (previous_ref, field.at[1]), (materials_ref, mats))[which]
        here = pl.ds(pl.multiple_of(strip * rows, rows), rows)
        return pltpu.make_async_copy(source.at[:, here, :], target.at[:, here, :], load_sem.at[which, strip])

    smalls = [
        pltpu.make_async_copy(source, target, small_sem.at[i])
        for i, (source, target) in enumerate(
            [
                (adm_hbm, adm_ref),
                (abs_hbm, abs_ref),
                (source_hbm, source_ref),
                (signal_hbm, signal_ref),
                (recv_hbm, recv_ref),
            ]
        )
    ]
    for small in smalls:
        small.start()
    for strip in range(STRIPS):
        for which in range(3):
            load(which, strip).start()

    barrier = pltpu.get_barrier_semaphore()

    def greet(hop, carry):
        pl.semaphore_signal(barrier, inc=1, device_id={"gx": lax.rem(me + hop, groups)}, device_id_type=pl.DeviceIdType.MESH)
        return carry

    lax.fori_loop(1, groups, greet, 0)
    pl.semaphore_wait(barrier, groups - 1)

    def send(step, side, strip, source):
        layer = layers - 1 if side == 0 else 0
        return pltpu.make_async_remote_copy(
            src_ref=source.at[layer, pl.ds(pl.multiple_of(strip * rows, rows), rows), :],
            dst_ref=halo.at[step, side, strip],
            send_sem=send_sem.at[step, side, strip],
            recv_sem=halo_sem.at[step, side, strip],
            device_id={"gx": me + 1 if side == 0 else me - 1},
            device_id_type=pl.DeviceIdType.MESH,
        )

    def on_sides(action):
        pl.when(has_right)(lambda: action(0))
        pl.when(has_left)(lambda: action(1))

    for strip in range(AHEAD):
        on_sides(lambda side: send(0, side, strip, pressure_ref).start())

    for small in smalls:
        small.wait()

    lane = lax.broadcasted_iota(jnp.int32, (8, 128), 1)
    outside_lane = lane // classes
    class_lane = lane - outside_lane * classes
    adm_lane = jnp.zeros((8, 128), jnp.float32)
    abs_lane = jnp.zeros((8, 128), jnp.float32)
    for m in range(classes):
        adm_lane = jnp.where(class_lane == m, adm_ref[m], adm_lane)
        abs_lane = jnp.where(class_lane == m, abs_ref[m], abs_lane)
    table = courant_sq / (1.0 + (0.5 * courant * outside_lane.astype(jnp.float32) * adm_lane + abs_lane))

    table_block = jnp.broadcast_to(table[0:1], (rows, 128))

    def fill(layer, row0):
        at_x = start_x + layer
        edge_x = jnp.where((at_x == 0) | (at_x == groups * layers - 1), classes, 0)
        row = row0 + lax.broadcasted_iota(jnp.int32, (rows, 128), 0)
        edge_xy = edge_x + jnp.where((row == 0) | (row == size_y - 1), classes, 0)
        for part in range(size_z // 128):
            cols = pl.ds(part * 128, 128)
            index = mats[layer, pl.ds(row0, rows), cols] + edge_xy
            col = part * 128 + lax.broadcasted_iota(jnp.int32, (rows, 128), 1)
            if part == 0 or part == size_z // 128 - 1:
                index = index + jnp.where((col == 0) | (col == size_z - 1), classes, 0)
            coef[layer, pl.ds(row0, rows), cols] = jnp.take_along_axis(table_block, index, axis=1, mode="promise_in_bounds")

    source = source_ref[0]
    source_x = source // (size_y * size_z) - start_x
    source_y = (source // size_z) % size_y
    source_z = source % size_z

    row_id = lax.broadcasted_iota(jnp.int32, (rows, 128), 0)
    col_id = lax.broadcasted_iota(jnp.int32, (rows, 128), 1)
    parts = size_z // 128
    mine[...] = jnp.zeros(mine.shape, jnp.float32)
    wide = mine.shape[1]
    mine_row = lax.broadcasted_iota(jnp.int32, mine.shape, 0)
    mine_col = lax.broadcasted_iota(jnp.int32, mine.shape, 1)
    lane_row = lax.broadcasted_iota(jnp.int32, (1, size_z), 1)

    def one_layer(step, now, then, strip, layer, low, high):
        row0 = pl.multiple_of(strip * rows, rows)
        here = pl.ds(row0, rows)
        push_x = jnp.where(source_x == layer, signal_ref[step], 0.0)
        above_row = field[now, layer, pl.ds(jnp.maximum(row0 - 1, 0), 1), :]
        below_row = field[now, layer, pl.ds(jnp.minimum(row0 + rows, size_y - 1), 1), :]
        cells = [field[now, layer, here, pl.ds(128 * part, 128)] for part in range(parts)]
        rights = [pltpu.roll(c, 1, 1) for c in cells]
        lefts = [pltpu.roll(c, 127, 1) for c in cells]
        for part in range(parts):
            cols = pl.ds(128 * part, 128)
            c = cells[part]
            above = above_row[:, 128 * part : 128 * part + 128]
            below = below_row[:, 128 * part : 128 * part + 128]
            down = pltpu.roll(c, 1, 0)
            down = jnp.concatenate([jnp.where(row_id[:8] == 0, above, down[:8]), down[8:]], axis=0)
            up = pltpu.roll(c, rows - 1, 0)
            up = jnp.concatenate([up[:-8], jnp.where(row_id[:8] == 7, below, up[-8:])], axis=0)
            total = low(part) + high(part)
            total = total + (down + up)
            total = total + jnp.where(col_id == 0, rights[part - 1] if part else c, rights[part])
            total = total + jnp.where(col_id == 127, lefts[part + 1] if part < parts - 1 else c, lefts[part])
            old = field[then, layer, here, cols]
            following = old + coef[layer, here, cols] * (total - 6.0 * old)
            push = jnp.where(lane_row[:, 128 * part : 128 * part + 128] == source_z, push_x, 0.0)
            following = following + jnp.where(row_id == source_y - row0, push, 0.0)
            field[then, layer, here, cols] = following

    def strip_body(step, strip):
        now = lax.rem(step, 2)
        then = 1 - now
        row0 = pl.multiple_of(strip * rows, rows)
        here = pl.ds(row0, rows)

        @pl.when(step == 0)
        def _():
            load(1, strip).wait()
            load(2, strip).wait()
            pl.when(strip < STRIPS - 1)(lambda: load(0, strip + 1).wait())
            for layer in range(layers):
                fill(layer, row0)
            pl.when(strip < STRIPS - AHEAD)(lambda: on_sides(lambda side: send(0, side, strip + AHEAD, pressure_ref).start()))

        def arrived(side):
            pltpu.make_async_copy(halo.at[step, side, strip], halo.at[step, side, strip], halo_sem.at[step, side, strip]).wait()

        pl.when(has_left)(lambda: arrived(0))
        pl.when(has_right)(lambda: arrived(1))
        @pl.when(step > 0)
        def _():
            on_sides(lambda side: send(step - 1, side, strip, field.at[then]).wait_send())

        def slab(layer):
            return lambda part: field[now, layer, here, pl.ds(128 * part, 128)]

        def side_low(part):
            cols = pl.ds(128 * part, 128)
            return jnp.where(has_left, halo[step, 0, strip, :, cols], field[now, 0, here, cols])

        def side_high(part):
            cols = pl.ds(128 * part, 128)
            return jnp.where(has_right, halo[step, 1, strip, :, cols], field[now, layers - 1, here, cols])

        for layer in [0, layers - 1] + list(range(1, layers - 1)):
            low = side_low if layer == 0 else slab(layer - 1)
            high = side_high if layer == layers - 1 else slab(layer + 1)
            one_layer(step, now, then, strip, layer, low, high)
            if layer == layers - 1:
                pl.when(step < steps - 1)(lambda: on_sides(lambda side: send(step + 1, side, strip, field.at[then]).start()))

    def step_body(step, carry):
        def inner(strip, c):
            strip_body(step, strip)
            return c

        lax.fori_loop(0, STRIPS, inner, 0)
        then = lax.rem(step + 1, 2)
        total = mine[...]
        for k in range(receivers // groups):
            slot = k * groups + me
            cell = recv_ref[slot]
            at_x = jnp.clip(cell // (size_y * size_z) - start_x, 0, layers - 1)
            at_y = (cell // size_z) % size_y
            at_z = cell % size_z
            line = field[then, at_x, pl.ds(at_y, 1), :]
            value = jnp.sum(jnp.where(lane_row == at_z, line, 0.0), axis=1, keepdims=True)
            total = total + jnp.where((mine_row == step) & (mine_col == slot), value, 0.0)
        mine[...] = total
        return carry

    load(0, 0).wait()
    lax.fori_loop(0, steps, step_body, 0)

    def gather_copy(hop):
        peer = lax.rem(me + hop, groups)
        return pltpu.make_async_remote_copy(
            src_ref=mine,
            dst_ref=gathered.at[hop],
            send_sem=gather_send.at[hop],
            recv_sem=gather_recv.at[hop],
            device_id={"gx": peer},
            device_id_type=pl.DeviceIdType.MESH,
        )

    def gather_start(hop, carry):
        gather_copy(hop).start()
        return carry

    lax.fori_loop(1, groups, gather_start, 0)

    for strip in range(STRIPS):
        on_sides(lambda side: send(steps - 1, side, strip, field.at[(steps - 1) % 2]).wait_send())

    def gather_add(hop, total):
        gather_copy(hop).wait()
        return total + gathered[hop]

    total = lax.fori_loop(1, groups, gather_add, mine[...])
    readings_ref[...] = total[0:steps, 0:receivers]


def write_kernel(field, readings, pressure_out, previous_out, readings_out, sems, small_sem):
    layers = pressure_out.shape[0]
    copies = [pltpu.make_async_copy(readings, readings_out, small_sem)]
    for layer in range(layers):
        for which, out in enumerate((pressure_out, previous_out)):
            copies.append(pltpu.make_async_copy(field.at[which, layer], out.at[layer], sems.at[which, layer]))
    for copy in copies:
        copy.start()
    for copy in copies:
        copy.wait()


def local(pressure, previous, materials, admittance, absorption, source_cell, signal, receivers):
    layers, size_y, size_z = pressure.shape
    groups = lax.axis_size("gx")
    steps = signal.shape[0]
    wide = -(-receivers.shape[0] // 128) * 128
    rows = size_y // STRIPS
    vmem = pl.BlockSpec(memory_space=pltpu.VMEM)
    hbm = pl.BlockSpec(memory_space=pltpu.HBM)
    field, readings = pl.pallas_call(
        functools.partial(kernel, groups, steps),
        out_shape=(
            pltpu.VMEM((2, layers, size_y, size_z), jnp.float32),
            pltpu.VMEM((steps, receivers.shape[0]), jnp.float32),
        ),
        in_specs=[hbm] * 8,
        out_specs=(vmem, vmem),
        scratch_shapes=[
            pltpu.SMEM(admittance.shape, jnp.float32),
            pltpu.SMEM(absorption.shape, jnp.float32),
            pltpu.SMEM(source_cell.shape, jnp.int32),
            pltpu.SMEM(signal.shape, jnp.float32),
            pltpu.SMEM(receivers.shape, jnp.int32),
            pltpu.SemaphoreType.DMA((5,)),
            pltpu.VMEM((layers, size_y, size_z), jnp.int32),
            pltpu.VMEM((layers, size_y, size_z), jnp.float32),
            pltpu.VMEM((steps, 2, STRIPS, rows, size_z), jnp.float32),
            pltpu.VMEM((8, wide), jnp.float32),
            pltpu.VMEM((groups, 8, wide), jnp.float32),
            pltpu.SemaphoreType.DMA((3, STRIPS)),
            pltpu.SemaphoreType.DMA((steps, 2, STRIPS)),
            pltpu.SemaphoreType.DMA((steps, 2, STRIPS)),
            pltpu.SemaphoreType.DMA((groups,)),
            pltpu.SemaphoreType.DMA((groups,)),
        ],
        compiler_params=pltpu.CompilerParams(
            collective_id=0, has_side_effects=True, vmem_limit_bytes=59 * 1024 * 1024
        ),
        name="steps",
    )(admittance, absorption, source_cell, signal, receivers, pressure, previous, materials)
    slab = jax.ShapeDtypeStruct((layers, size_y, size_z), jnp.float32)
    return pl.pallas_call(
        write_kernel,
        out_shape=(slab, slab, jax.ShapeDtypeStruct(readings.shape, jnp.float32)),
        in_specs=[pl.BlockSpec(memory_space=pl.ANY)] * 2,
        out_specs=(hbm, hbm, hbm),
        scratch_shapes=[pltpu.SemaphoreType.DMA((2, layers)), pltpu.SemaphoreType.DMA],
        compiler_params=pltpu.CompilerParams(vmem_limit_bytes=1024 * 1024),
        name="write",
    )(field, readings)


def solution(mesh):
    slab = P(("room", "gx"), None, None)
    return jax.shard_map(
        local,
        mesh=mesh,
        in_specs=(slab, slab, slab, P("room"), P("room"), P("room"), P("room"), P("room")),
        out_specs=(slab, slab, P("room", None)),
        check_vma=False,
    )
```

```python
import functools

import jax
import jax.numpy as jnp
from jax import lax
from jax.experimental import pallas as pl
from jax.experimental.pallas import tpu as pltpu
from jax.sharding import PartitionSpec as P

courant = 0.5773502691896258
courant_sq = 1.0 / 3.0

STRIPS = 2
AHEAD = 2


def kernel(
    groups,
    steps,
    adm_hbm,
    abs_hbm,
    source_hbm,
    signal_hbm,
    recv_hbm,
    pressure_ref,
    previous_ref,
    materials_ref,
    field,
    readings_ref,
    adm_ref,
    abs_ref,
    source_ref,
    signal_ref,
    recv_ref,
    small_sem,
    mats,
    coef,
    halo,
    mine,
    gathered,
    load_sem,
    send_sem,
    halo_sem,
    gather_send,
    gather_recv,
):
    layers, size_y, size_z = pressure_ref.shape
    rows = size_y // STRIPS
    receivers = recv_ref.shape[0]
    classes = adm_ref.shape[0]
    me = lax.axis_index("gx")
    start_x = me * layers
    has_left = me > 0
    has_right = me < groups - 1

    barrier = pltpu.get_barrier_semaphore()

    def greet(hop, carry):
        pl.semaphore_signal(barrier, inc=1, device_id={"gx": lax.rem(me + hop, groups)}, device_id_type=pl.DeviceIdType.MESH)
        return carry

    lax.fori_loop(1, groups, greet, 0, unroll=groups <= 16)
    def load(which, strip):
        source, target = ((pressure_ref, field.at[0]), (previous_ref, field.at[1]), (materials_ref, mats))[which]
        here = pl.ds(pl.multiple_of(strip * rows, rows), rows)
        return pltpu.make_async_copy(source.at[:, here, :], target.at[:, here, :], load_sem.at[which, strip])

    smalls = [
        pltpu.make_async_copy(source, target, small_sem.at[i])
        for i, (source, target) in enumerate(
            [
                (adm_hbm, adm_ref),
                (abs_hbm, abs_ref),
                (source_hbm, source_ref),
                (signal_hbm, signal_ref),
                (recv_hbm, recv_ref),
            ]
        )
    ]
    for small in smalls:
        small.start()
    for strip in range(STRIPS):
        for which in range(3):
            load(which, strip).start()

    pl.semaphore_wait(barrier, groups - 1)

    def send(step, side, strip, source):
        layer = layers - 1 if side == 0 else 0
        return pltpu.make_async_remote_copy(
            src_ref=source.at[layer, pl.ds(pl.multiple_of(strip * rows, rows), rows), :],
            dst_ref=halo.at[step, side, strip],
            send_sem=send_sem.at[step, side, strip],
            recv_sem=halo_sem.at[step, side, strip],
            device_id={"gx": me + 1 if side == 0 else me - 1},
            device_id_type=pl.DeviceIdType.MESH,
        )

    def on_sides(action):
        pl.when(has_right)(lambda: action(0))
        pl.when(has_left)(lambda: action(1))

    for strip in range(AHEAD):
        on_sides(lambda side: send(0, side, strip, pressure_ref).start())

    for small in smalls:
        small.wait()

    lane = lax.broadcasted_iota(jnp.int32, (8, 128), 1)
    outside_lane = lane // classes
    class_lane = lane - outside_lane * classes
    adm_lane = jnp.zeros((8, 128), jnp.float32)
    abs_lane = jnp.zeros((8, 128), jnp.float32)
    for m in range(classes):
        adm_lane = jnp.where(class_lane == m, adm_ref[m], adm_lane)
        abs_lane = jnp.where(class_lane == m, abs_ref[m], abs_lane)
    table = courant_sq / (1.0 + (0.5 * courant * outside_lane.astype(jnp.float32) * adm_lane + abs_lane))

    table_block = jnp.broadcast_to(table[0:1], (rows, 128))

    def fill(layer, row0):
        at_x = start_x + layer
        edge_x = jnp.where((at_x == 0) | (at_x == groups * layers - 1), classes, 0)
        row = row0 + lax.broadcasted_iota(jnp.int32, (rows, 128), 0)
        edge_xy = edge_x + jnp.where((row == 0) | (row == size_y - 1), classes, 0)
        for part in range(size_z // 128):
            cols = pl.ds(part * 128, 128)
            index = mats[layer, pl.ds(row0, rows), cols] + edge_xy
            col = part * 128 + lax.broadcasted_iota(jnp.int32, (rows, 128), 1)
            if part == 0 or part == size_z // 128 - 1:
                index = index + jnp.where((col == 0) | (col == size_z - 1), classes, 0)
            coef[layer, pl.ds(row0, rows), cols] = jnp.take_along_axis(table_block, index, axis=1, mode="promise_in_bounds")

    source = source_ref[0, 0]
    source_x = source // (size_y * size_z) - start_x
    source_y = (source // size_z) % size_y
    source_z = source % size_z

    row_id = lax.broadcasted_iota(jnp.int32, (rows, 128), 0)
    col_id = lax.broadcasted_iota(jnp.int32, (rows, 128), 1)
    parts = size_z // 128
    mine[...] = jnp.zeros(mine.shape, jnp.float32)
    wide = mine.shape[1]
    mine_row = lax.broadcasted_iota(jnp.int32, mine.shape, 0)
    mine_col = lax.broadcasted_iota(jnp.int32, mine.shape, 1)
    lane_row = lax.broadcasted_iota(jnp.int32, (1, size_z), 1)

    def one_layer(step, now, then, strip, layer, low, high):
        row0 = pl.multiple_of(strip * rows, rows)
        here = pl.ds(row0, rows)
        push_x = jnp.where(source_x == layer, signal_ref[step], 0.0)
        above_row = field[now, layer, pl.ds(jnp.maximum(row0 - 1, 0), 1), :]
        below_row = field[now, layer, pl.ds(jnp.minimum(row0 + rows, size_y - 1), 1), :]
        cells = [field[now, layer, here, pl.ds(128 * part, 128)] for part in range(parts)]
        rights = [pltpu.roll(c, 1, 1) for c in cells]
        lefts = [pltpu.roll(c, 127, 1) for c in cells]
        for part in range(parts):
            cols = pl.ds(128 * part, 128)
            c = cells[part]
            above = above_row[:, 128 * part : 128 * part + 128]
            below = below_row[:, 128 * part : 128 * part + 128]
            down = pltpu.roll(c, 1, 0)
            down = jnp.concatenate([jnp.where(row_id[:8] == 0, above, down[:8]), down[8:]], axis=0)
            up = pltpu.roll(c, rows - 1, 0)
            up = jnp.concatenate([up[:-8], jnp.where(row_id[:8] == 7, below, up[-8:])], axis=0)
            total = low(part) + high(part)
            total = total + (down + up)
            total = total + jnp.where(col_id == 0, rights[part - 1] if part else c, rights[part])
            total = total + jnp.where(col_id == 127, lefts[part + 1] if part < parts - 1 else c, lefts[part])
            old = field[then, layer, here, cols]
            following = old + coef[layer, here, cols] * (total - 6.0 * old)
            push = jnp.where(lane_row[:, 128 * part : 128 * part + 128] == source_z, push_x, 0.0)
            following = following + jnp.where(row_id == source_y - row0, push, 0.0)
            field[then, layer, here, cols] = following

    def strip_body(step, strip):
        now = lax.rem(step, 2)
        then = 1 - now
        row0 = pl.multiple_of(strip * rows, rows)
        here = pl.ds(row0, rows)

        @pl.when(step == 0)
        def _():
            load(1, strip).wait()
            load(2, strip).wait()
            pl.when(strip < STRIPS - 1)(lambda: load(0, strip + 1).wait())
            for layer in range(layers):
                fill(layer, row0)
            pl.when(strip < STRIPS - AHEAD)(lambda: on_sides(lambda side: send(0, side, strip + AHEAD, pressure_ref).start()))

        def arrived(side):
            pltpu.make_async_copy(halo.at[step, side, strip], halo.at[step, side, strip], halo_sem.at[step, side, strip]).wait()

        def receive():
            pl.when(has_left)(lambda: arrived(0))
            pl.when(has_right)(lambda: arrived(1))
            @pl.when(step > 0)
            def _():
                on_sides(lambda side: send(step - 1, side, strip, field.at[then]).wait_send())

        def slab(layer):
            return lambda part: field[now, layer, here, pl.ds(128 * part, 128)]

        def side_low(part):
            cols = pl.ds(128 * part, 128)
            return jnp.where(has_left, halo[step, 0, strip, :, cols], field[now, 0, here, cols])

        def side_high(part):
            cols = pl.ds(128 * part, 128)
            return jnp.where(has_right, halo[step, 1, strip, :, cols], field[now, layers - 1, here, cols])

        for layer in list(range(1, layers - 1)) + [0, layers - 1]:
            if layer == 0:
                receive()
            low = side_low if layer == 0 else slab(layer - 1)
            high = side_high if layer == layers - 1 else slab(layer + 1)
            one_layer(step, now, then, strip, layer, low, high)
            if layer == layers - 1:
                pl.when(step < steps - 1)(lambda: on_sides(lambda side: send(step + 1, side, strip, field.at[then]).start()))

    def step_body(step, carry):
        def inner(strip, c):
            strip_body(step, strip)
            return c

        lax.fori_loop(0, STRIPS, inner, 0)
        then = lax.rem(step + 1, 2)
        total = mine[...]
        for k in range(receivers // groups):
            slot = k * groups + me
            cell = recv_ref[slot]
            at_x = jnp.clip(cell // (size_y * size_z) - start_x, 0, layers - 1)
            at_y = (cell // size_z) % size_y
            at_z = cell % size_z
            line = field[then, at_x, pl.ds(at_y, 1), :]
            value = jnp.sum(jnp.where(lane_row == at_z, line, 0.0), axis=1, keepdims=True)
            total = total + jnp.where((mine_row == step) & (mine_col == slot), value, 0.0)
        mine[...] = total
        return carry

    load(0, 0).wait()
    lax.fori_loop(0, steps, step_body, 0)

    def gather_copy(hop):
        peer = lax.rem(me + hop, groups)
        return pltpu.make_async_remote_copy(
            src_ref=mine,
            dst_ref=gathered.at[hop],
            send_sem=gather_send.at[hop],
            recv_sem=gather_recv.at[hop],
            device_id={"gx": peer},
            device_id_type=pl.DeviceIdType.MESH,
        )

    def gather_start(hop, carry):
        gather_copy(hop).start()
        return carry

    lax.fori_loop(1, groups, gather_start, 0, unroll=groups <= 16)

    for strip in range(STRIPS):
        on_sides(lambda side: send(steps - 1, side, strip, field.at[(steps - 1) % 2]).wait_send())

    def gather_wait(hop, carry):
        gather_copy(hop).wait()
        return carry

    lax.fori_loop(1, groups, gather_wait, 0, unroll=groups <= 16)
    total = lax.fori_loop(1, groups, lambda hop, total: total + gathered[hop], mine[...], unroll=groups <= 16)
    readings_ref[...] = total[0:steps, 0:receivers]


def write_kernel(field, readings, pressure_out, previous_out, readings_out, sems, small_sem):
    layers = pressure_out.shape[0]
    copies = [pltpu.make_async_copy(readings, readings_out, small_sem)]
    for layer in range(layers):
        for which, out in enumerate((pressure_out, previous_out)):
            copies.append(pltpu.make_async_copy(field.at[which, layer], out.at[layer], sems.at[which, layer]))
    for copy in copies:
        copy.start()
    for copy in copies:
        copy.wait()


def local(pressure, previous, materials, admittance, absorption, source_cell, signal, receivers):
    layers, size_y, size_z = pressure.shape
    groups = lax.axis_size("gx")
    steps = signal.shape[0]
    wide = -(-receivers.shape[0] // 128) * 128
    rows = size_y // STRIPS
    vmem = pl.BlockSpec(memory_space=pltpu.VMEM)
    hbm = pl.BlockSpec(memory_space=pltpu.HBM)
    field, readings = pl.pallas_call(
        functools.partial(kernel, groups, steps),
        out_shape=(
            pltpu.VMEM((2, layers, size_y, size_z), jnp.float32),
            pltpu.VMEM((steps, receivers.shape[0]), jnp.float32),
        ),
        in_specs=[hbm] * 8,
        out_specs=(vmem, vmem),
        scratch_shapes=[
            pltpu.SMEM(admittance.shape, jnp.float32),
            pltpu.SMEM(absorption.shape, jnp.float32),
            pltpu.SMEM((1, 1), jnp.int32),
            pltpu.SMEM(signal.shape, jnp.float32),
            pltpu.SMEM(receivers.shape, jnp.int32),
            pltpu.SemaphoreType.DMA((5,)),
            pltpu.VMEM((layers, size_y, size_z), jnp.int32),
            pltpu.VMEM((layers, size_y, size_z), jnp.float32),
            pltpu.VMEM((steps, 2, STRIPS, rows, size_z), jnp.float32),
            pltpu.VMEM((8, wide), jnp.float32),
            pltpu.VMEM((groups, 8, wide), jnp.float32),
            pltpu.SemaphoreType.DMA((3, STRIPS)),
            pltpu.SemaphoreType.DMA((steps, 2, STRIPS)),
            pltpu.SemaphoreType.DMA((steps, 2, STRIPS)),
            pltpu.SemaphoreType.DMA((groups,)),
            pltpu.SemaphoreType.DMA((groups,)),
        ],
        compiler_params=pltpu.CompilerParams(
            collective_id=0, has_side_effects=True, vmem_limit_bytes=59 * 1024 * 1024
        ),
        name="steps",
    )(admittance, absorption, source_cell.reshape(1, 1), signal, receivers, pressure, previous, materials)
    slab = jax.ShapeDtypeStruct((layers, size_y, size_z), jnp.float32)
    return pl.pallas_call(
        write_kernel,
        out_shape=(slab, slab, jax.ShapeDtypeStruct(readings.shape, jnp.float32)),
        in_specs=[pl.BlockSpec(memory_space=pl.ANY)] * 2,
        out_specs=(hbm, hbm, hbm),
        scratch_shapes=[pltpu.SemaphoreType.DMA((2, layers)), pltpu.SemaphoreType.DMA],
        compiler_params=pltpu.CompilerParams(vmem_limit_bytes=1024 * 1024),
        name="write",
    )(field, readings)


def solution(mesh):
    slab = P(("room", "gx"), None, None)
    return jax.shard_map(
        local,
        mesh=mesh,
        in_specs=(slab, slab, slab, P("room"), P("room"), P("room"), P("room"), P("room")),
        out_specs=(slab, slab, P("room", None)),
        check_vma=False,
    )
```
